32 devices in a mesh: groups: 2 (over x), adapt: 16 (over z, y, core).
Axes of the slice: x: 2, y: 2, z: 4, core: 2. Of those that a mesh axis runs over, the one named last changes fastest.
Arguments:
- tokens: bfloat16 [16384, 5120], P(('groups', 'adapt')), parts along dimension 0, may hold values from -6 to 6
- lengths: int32 [32, 8], P(('groups', 'adapt')), parts along dimension 0, may hold values from 1 to 256, 512 in all within a row
- active: int32 [32, 4], P(('groups', 'adapt')), parts along dimension 0, may hold values from 0 to 31
- program_adapter_slot: int32 [32, 8], P(('groups', 'adapt')), parts along dimension 0, may hold values from 0 to 3
- base_weight: bfloat16 [5120, 512], replicated, may hold values from -0.078125 to 0.078125
- adapter_down: bfloat16 [64, 327680], P('groups', 'adapt'), parts along dimension 0, may hold values from -0.078125 to 0.078125
- adapter_up: bfloat16 [64, 32768], P('groups', 'adapt'), parts along dimension 0, may hold values from -0.75 to 0.75
Outputs:
- values: bfloat16 [16384, 512], P(('groups', 'adapt')), parts along dimension 0
The draws below stay inside these ranges and needn't reach their ends.
There are 2 independent parts, one for each index of `groups`. The reference program is written for one: setup_inputs(seed, part) draws one part's arguments, and reference() takes and returns one part's arrays. A program takes and returns all parts, laid end to end along the dimension named above; an argument that names none is the same for every part. Nothing has to cross between parts.
Inputs may be any that keep to these rules, and one draw needn't show every extreme that they name: Each device's lengths sum to 512; the longest program of each device has 256 rows. `active`: ids of stored adapters; some are common.
All inputs are finite; a program needn't handle non-finite values.
Results may differ from the reference program's by a relative error of at most 0.0075.
Values may be sent and summed in bfloat16 or wider, within the bound.
A program may use at most 128 MiB of HBM per device.

```python
import math
import jax
import jax.numpy as jnp
import numpy as np
from jax import lax

D = 5120
KV = 512
R = 64
ROWS_DEV = 512
PROG_DEV = 8
ACTIVE = 4
MOST = 256
ADAPTER_COUNT = 32
ROWS = 8192
N_ADAPT = 16


def touch_ends(result, own_key, smallest, high):
    extent = result.shape
    spot = [jax.random.randint(jax.random.fold_in(own_key, axis), (), 0, extent[axis]) for axis in range(len(extent))]
    result = result.at[tuple(spot)].set(smallest)
    longest = extent.index(max(extent))
    spot[longest] = (spot[longest] + 1) % extent[longest]
    return result.at[tuple(spot)].set(high)


def level_of(own_key, dims, split, smallest, largest):
    gain = 1.0
    for axis_at, blocks in split:
        heights = jax.random.uniform(jax.random.fold_in(jax.random.fold_in(own_key, 6), axis_at), (blocks,), jnp.float32, smallest / len(split), largest / len(split))
        gain = gain * jnp.repeat(jnp.exp(heights), dims[axis_at] // blocks).reshape((-1,) + (1,) * (len(dims) - 1 - axis_at))
    return gain


def rank_bounds(count, lean):
    weights = [(1 << 20) // math.isqrt(rank ** lean) + 1 for rank in range(1, count + 1)]
    deviation = 1 + sum(weights) // (1 << 30)
    return np.cumsum(np.array([max(1, weight // deviation) for weight in weights]))


def skewed_ids(rng, extent, number_of, lean):
    grid = rank_bounds(number_of, lean)
    ticket = jax.random.randint(jax.random.fold_in(rng, 1), extent, 0, int(grid[number_of - 1]))
    grade = jnp.searchsorted(jnp.asarray(grid, jnp.int32), ticket, side="right")
    return jax.random.permutation(jax.random.fold_in(rng, 2), number_of)[grade].astype(jnp.int32)


def profile(amount, total, most, skew):
    weights = [(1 << 20) // math.isqrt(grade ** skew) + 1 for grade in range(2, amount + 1)]
    surplus, counts = total - most - (amount - 1), [1] * (amount - 1)
    while surplus > 0:
        movable = [i for i in range(amount - 1) if counts[i] < most]
        mass, left = sum([weights[i] for i in movable]), surplus
        for i in movable:
            addition = min(most - counts[i], max(1, left * weights[i] // mass), surplus)
            counts[i] = counts[i] + addition
            surplus = surplus - addition
    return np.array([most] + counts)


def uneven_parts(rng, amount, total, reach, lean):
    if amount == 2:
        one = jax.random.randint(rng, (), max(1, total - reach), min(reach, total - 1) + 1)
        return jnp.stack([one, total - one])
    sizes = jnp.asarray(profile(amount, total, reach, lean), jnp.int32)
    twos = (amount - 1) // 2
    donor, taker = sizes[1:1 + 2 * twos:2], sizes[2:2 + 2 * twos:2]
    slack = jnp.minimum(donor - 1, reach - taker)
    passed = jax.random.randint(jax.random.fold_in(rng, 1), (twos,), 0, 1 << 20) % (slack + 1)
    sizes = sizes.at[1:1 + 2 * twos:2].set(donor - passed).at[2:2 + 2 * twos:2].set(taker + passed)
    return sizes[jax.random.permutation(jax.random.fold_in(rng, 2), amount)]


def normal_values(key, shape, deviation, limit, split=(), kind=jnp.bfloat16):
    entries = jax.random.normal(key, shape, jnp.float32) * deviation
    if len(split) > 0:
        entries = level_of(key, shape, split, -0.22, 0.18) * entries
    return jnp.clip(entries, min=-limit, max=limit).astype(kind)


def setup_inputs(seed: int = 0, part: int = 0) -> dict:
    streams_of = jax.random.split(jax.random.key(seed), 8)
    part_splits = jax.random.split(jax.random.fold_in(streams_of[7], part), 8)
    return {
        "tokens": normal_values(part_splits[0], (ROWS, D), 1.0, 6.0, ((0, 16),)),
        "lengths": jax.vmap(lambda own: uneven_parts(own, PROG_DEV, ROWS_DEV, MOST, 2))(jax.random.split(part_splits[1], N_ADAPT)).reshape((N_ADAPT, PROG_DEV)).astype(jnp.int32),
        "active": touch_ends(skewed_ids(part_splits[2], (N_ADAPT, ACTIVE), ADAPTER_COUNT, 2), jax.random.fold_in(part_splits[2], 3), 0, ADAPTER_COUNT - 1).astype(jnp.int32),
        "program_adapter_slot": touch_ends(jax.random.randint(part_splits[3], (N_ADAPT, PROG_DEV), 0, ACTIVE), jax.random.fold_in(part_splits[3], 1), 0, ACTIVE - 1).astype(jnp.int32),
        "base_weight": normal_values(streams_of[4], (D, KV), D ** -0.5, 0.078125),
        "adapter_down": normal_values(part_splits[5], (ADAPTER_COUNT, D * R), D ** -0.5, 0.078125, ((1, 16),)),
        "adapter_up": normal_values(part_splits[6], (ADAPTER_COUNT, KV * R), R ** -0.5, 0.75, ((1, 16),)),
    }


adapter_scale = 2.0


def slot_onehot(program_lengths, program_slots, row_count, slot_count):
    programs = program_lengths.shape[0]
    program_ends = jnp.cumsum(program_lengths)
    position = lax.broadcasted_iota(jnp.int32, (row_count, programs), 0)
    program = jnp.sum((position >= program_ends[None, :]).astype(jnp.int32), axis=1)
    owner_mask = (program[:, None] == lax.broadcasted_iota(jnp.int32, (row_count, programs), 1)).astype(jnp.int32)
    row_slot = jnp.sum(owner_mask * program_slots[None, :], axis=1)
    return (row_slot[:, None] == lax.broadcasted_iota(jnp.int32, (row_count, slot_count), 1)).astype(jnp.float32)


def reference(tokens, lengths, active, program_adapter_slot, base_weight, adapter_down, adapter_up):
    def block(block_index):
        here = lax.dynamic_slice_in_dim(tokens, block_index * ROWS_DEV, ROWS_DEV, 0)
        selector = slot_onehot(lengths[block_index], program_adapter_slot[block_index], ROWS_DEV, ACTIVE)
        down_mats = adapter_down[active[block_index]].reshape(ACTIVE, D, R).astype(jnp.float32)
        up_mats = adapter_up[active[block_index]].reshape(ACTIVE, KV, R).astype(jnp.float32)
        wide = jnp.einsum("td,jdr->tjr", here.astype(jnp.float32), down_mats)
        low_rank = jnp.sum(selector[:, :, None] * wide, axis=1).astype(jnp.bfloat16)
        masked = selector[:, :, None] * low_rank.astype(jnp.float32)[:, None, :]
        adapter_update = jnp.einsum("tjr,jkr->tk", masked, up_mats)
        frozen_output = jnp.dot(here, base_weight, preferred_element_type=jnp.float32)
        return (frozen_output + adapter_scale * adapter_update).astype(jnp.bfloat16)

    blocks = lax.map(block, jnp.arange(N_ADAPT, dtype=jnp.int32))
    return blocks.reshape(ROWS_DEV * N_ADAPT, KV)
```

```python
import functools
import math

import jax
import jax.numpy as jnp
from jax import lax
from jax.experimental import pallas as pl
from jax.experimental.pallas import tpu as pltpu
from jax.sharding import PartitionSpec as P

D = 5120
KV = 512
R = 64
ACTIVE = 4
LANES = 128

adapter_scale = 2.0
MESH = pl.DeviceIdType.MESH


def kernel(
    n, down_rows, up_rows,
    active_ref, lengths_ref, slots_ref, tokens_hbm, base_hbm, store_ref, out_ref,
    tokens, base, ids_vmem, ids, send, recv, wide_weight, up_weight, total, wide,
    id_send_sem, id_recv_sem, id_sem, send_sem, recv_sem, token_sem, base_sem,
):
    me = lax.axis_index("adapt")
    d_local = 2 * down_rows
    group = LANES // math.gcd(LANES, d_local)
    groups = n // group
    half_groups = groups // 2
    span = group * d_local
    my_group, my_core = me // group, me % group
    my_half = my_group // half_groups
    row_count = out_ref.shape[0]

    token_copy = pltpu.make_async_copy(tokens_hbm, tokens, token_sem)
    base_copy = pltpu.make_async_copy(base_hbm, base, base_sem)
    token_copy.start()
    base_copy.start()

    barrier = pltpu.get_barrier_semaphore()

    def greet(k, _):
        pl.semaphore_signal(barrier, inc=1, device_id={"adapt": (me + k) % n}, device_id_type=MESH)
        return 0

    lax.fori_loop(1, n, greet, 0)
    pl.semaphore_wait(barrier, n - 1)

    def id_copy(k, origin):
        return pltpu.make_async_remote_copy(
            src_ref=active_ref, dst_ref=ids_vmem.at[origin],
            send_sem=id_send_sem.at[k], recv_sem=id_recv_sem.at[origin],
            device_id={"adapt": (me + k) % n}, device_id_type=MESH,
        )

    def send_ids(k, _):
        id_copy(k, me).start()
        return 0

    def await_ids(k, _):
        id_copy(k, (me + k) % n).wait_recv()
        return 0

    lax.fori_loop(1, n, send_ids, 0)
    ids_vmem[me] = active_ref[...]
    lax.fori_loop(1, n, await_ids, 0)
    to_scalars = pltpu.make_async_copy(ids_vmem, ids, id_sem)
    to_scalars.start()
    to_scalars.wait()

    def piece_copy(target, origin):
        return pltpu.make_async_remote_copy(
            src_ref=send.at[target], dst_ref=recv.at[origin],
            send_sem=send_sem.at[target], recv_sem=recv_sem.at[origin],
            device_id={"adapt": target}, device_id_type=MESH,
        )

    def send_group(t, _):
        other = (my_half + t + 1) % 2
        partner_group = other * half_groups + (my_group + t // 2) % half_groups

        def send_core(c, _):
            target = partner_group * group + (my_core + c) % group

            @pl.when(target != me)
            def _():
                for j in range(ACTIVE):
                    send[target, j] = store_ref[ids[target, 0, j]]
                piece_copy(target, me).start()

            return 0

        return lax.fori_loop(0, group, send_core, 0)

    lax.fori_loop(0, groups, send_group, 0)
    for j in range(ACTIVE):
        recv[me, j] = store_ref[ids[me, 0, j]]

    token_copy.wait()
    base_copy.wait()
    total[...] = jnp.zeros_like(total)
    wide[...] = jnp.zeros_like(wide)

    def base_step(g, _):
        at = pl.ds(pl.multiple_of(g * span, LANES), span)
        total[...] += jnp.dot(tokens[:, at], base[at, :], preferred_element_type=jnp.float32)
        return 0

    lax.fori_loop(0, groups, base_step, 0)

    rows = down_rows + up_rows
    twice = (
        lax.broadcasted_iota(jnp.int32, (2 * rows, rows), 0) // 2
        == lax.broadcasted_iota(jnp.int32, (2 * rows, rows), 1)
    ).astype(jnp.bfloat16)
    parity = (
        lax.broadcasted_iota(jnp.int32, (2 * rows, ACTIVE * LANES), 0) % 2
        == (lax.broadcasted_iota(jnp.int32, (2 * rows, ACTIVE * LANES), 1) % LANES) // R
    )

    def take_group(t, _):
        half = (my_half + t) % 2
        from_group = half * half_groups + (my_group - t // 2 + half_groups) % half_groups

        def take_core(c, _):
            origin = from_group * group + c

            @pl.when(origin != me)
            def _():
                piece_copy(origin, origin).wait_recv()

            packed = jnp.concatenate([recv[origin, j] for j in range(ACTIVE)], axis=1)
            spread = jnp.dot(twice, packed, preferred_element_type=jnp.float32)
            spread = jnp.where(parity, spread, 0.0)
            wide_weight[pl.ds(pl.multiple_of(c * d_local, 16), d_local), :] = spread[:d_local].astype(jnp.bfloat16)
            up_weight[pl.ds(pl.multiple_of(origin * 2 * up_rows, 8), 2 * up_rows), :] = spread[d_local:]
            return 0

        lax.fori_loop(0, group, take_core, 0)
        at = pl.ds(pl.multiple_of(from_group * span, LANES), span)
        wide[...] += jnp.dot(tokens[:, at], wide_weight[...], preferred_element_type=jnp.float32)
        return 0

    lax.fori_loop(0, groups, take_group, 0)

    position = lax.broadcasted_iota(jnp.int32, (row_count, LANES), 0)
    row_slot = jnp.zeros((row_count, LANES), jnp.int32)
    begin = jnp.int32(0)
    for p in range(lengths_ref.shape[1]):
        end = begin + lengths_ref[0, p]
        inside = jnp.logical_and(position >= begin, position < end)
        row_slot = jnp.where(inside, slots_ref[0, p], row_slot)
        begin = end
    picked = []
    for j in range(ACTIVE):
        mine = wide[:, j * LANES:(j + 1) * LANES]
        low = mine + pltpu.roll(mine, R, 1)
        picked.append(jnp.where(row_slot == j, low, 0.0).astype(jnp.bfloat16))
    low_rank = jnp.concatenate(picked, axis=1)
    delta = lax.dot_general(
        low_rank, up_weight[...].astype(jnp.bfloat16),
        (((1,), (1,)), ((), ())), preferred_element_type=jnp.float32,
    )
    out_ref[...] = (total[...] + adapter_scale * delta).astype(out_ref.dtype)

    def finish(k, _):
        target = (me + k) % n
        id_copy(k, me).wait_send()
        piece_copy(target, me).wait_send()
        return 0

    lax.fori_loop(1, n, finish, 0)


def shards(tokens, lengths, active, program_adapter_slot, base_weight, adapter_down, adapter_up):
    n = lax.axis_size("adapt")
    row_count = tokens.shape[0]
    stored = adapter_down.shape[0]
    down_rows = adapter_down.shape[1] // LANES
    up_rows = adapter_up.shape[1] // LANES
    rows = down_rows + up_rows
    store = jnp.concatenate([adapter_down, adapter_up], axis=1).reshape(stored, rows, LANES)
    slot_list = jnp.pad(active, ((0, 0), (0, LANES - ACTIVE)))
    d_local = 2 * down_rows
    group = LANES // math.gcd(LANES, d_local)
    vmem, smem, hbm = pltpu.VMEM, pltpu.SMEM, pl.ANY
    width = ACTIVE * LANES
    return pl.pallas_call(
        functools.partial(kernel, n, down_rows, up_rows),
        out_shape=jax.ShapeDtypeStruct((row_count, KV), jnp.bfloat16),
        in_specs=[pl.BlockSpec(memory_space=s) for s in (vmem, smem, smem, hbm, hbm, vmem)],
        out_specs=pl.BlockSpec(memory_space=vmem),
        scratch_shapes=[
            pltpu.VMEM((row_count, D), jnp.bfloat16),
            pltpu.VMEM((D, KV), jnp.bfloat16),
            pltpu.VMEM((n, 1, LANES), jnp.int32),
            pltpu.SMEM((n, 1, LANES), jnp.int32),
            pltpu.VMEM((n, ACTIVE, rows, LANES), jnp.bfloat16),
            pltpu.VMEM((n, ACTIVE, rows, LANES), jnp.bfloat16),
            pltpu.VMEM((group * d_local, width), jnp.bfloat16),
            pltpu.VMEM((KV, width), jnp.float32),
            pltpu.VMEM((row_count, KV), jnp.float32),
            pltpu.VMEM((row_count, width), jnp.float32),
            pltpu.SemaphoreType.DMA((n,)),
            pltpu.SemaphoreType.DMA((n,)),
            pltpu.SemaphoreType.DMA,
            pltpu.SemaphoreType.DMA((n,)),
            pltpu.SemaphoreType.DMA((n,)),
            pltpu.SemaphoreType.DMA,
            pltpu.SemaphoreType.DMA,
        ],
        compiler_params=pltpu.CompilerParams(
            collective_id=0, has_side_effects=True, vmem_limit_bytes=48 * 1024 * 1024
        ),
    )(slot_list, lengths, program_adapter_slot, tokens, base_weight, store)


def solution(mesh):
    in_specs = (
        P(("groups", "adapt"), None),
        P(("groups", "adapt"), None),
        P(("groups", "adapt"), None),
        P(("groups", "adapt"), None),
        P(),
        P("groups", "adapt"),
        P("groups", "adapt"),
    )
    out_specs = P(("groups", "adapt"), None)
    return jax.shard_map(shards, mesh=mesh, in_specs=in_specs, out_specs=out_specs, check_vma=False)
```

```python
import functools
import math

import jax
import jax.numpy as jnp
from jax import lax
from jax.experimental import pallas as pl
from jax.experimental.pallas import tpu as pltpu
from jax.sharding import PartitionSpec as P

D = 5120
KV = 512
R = 64
ACTIVE = 4
LANES = 128

adapter_scale = 2.0
MESH = pl.DeviceIdType.MESH


def direct_kernel(
    n, down_rows, up_rows,
    active_ref, lengths_ref, slots_ref, tokens_hbm, base_hbm, store_ref, out_ref,
    tokens, base, ids_vmem, ids, send, recv, wide_weight, up_weight, total, wide,
    id_send_sem, id_recv_sem, id_sem, send_sem, recv_sem, token_sem, base_sem,
):
    me = lax.axis_index("adapt")
    d_local = 2 * down_rows
    group = LANES // math.gcd(LANES, d_local)
    groups = n // group
    half_groups = groups // 2
    span = group * d_local
    my_group, my_core = me // group, me % group
    my_half = my_group // half_groups
    row_count = out_ref.shape[0]

    token_copy = pltpu.make_async_copy(tokens_hbm, tokens, token_sem)
    base_copy = pltpu.make_async_copy(base_hbm, base, base_sem)
    token_copy.start()
    base_copy.start()

    barrier = pltpu.get_barrier_semaphore()

    def greet(k, _):
        pl.semaphore_signal(barrier, inc=1, device_id={"adapt": (me + k) % n}, device_id_type=MESH)
        return 0

    lax.fori_loop(1, n, greet, 0)
    pl.semaphore_wait(barrier, n - 1)

    def id_copy(k, origin):
        return pltpu.make_async_remote_copy(
            src_ref=active_ref, dst_ref=ids_vmem.at[origin],
            send_sem=id_send_sem.at[k], recv_sem=id_recv_sem.at[origin],
            device_id={"adapt": (me + k) % n}, device_id_type=MESH,
        )

    def send_ids(k, _):
        id_copy(k, me).start()
        return 0

    def await_ids(k, _):
        id_copy(k, (me + k) % n).wait_recv()
        return 0

    lax.fori_loop(1, n, send_ids, 0)
    ids_vmem[me] = active_ref[...]
    lax.fori_loop(1, n, await_ids, 0)
    to_scalars = pltpu.make_async_copy(ids_vmem, ids, id_sem)
    to_scalars.start()
    to_scalars.wait()

    def piece_copy(target, origin):
        return pltpu.make_async_remote_copy(
            src_ref=send.at[target], dst_ref=recv.at[origin],
            send_sem=send_sem.at[target], recv_sem=recv_sem.at[origin],
            device_id={"adapt": target}, device_id_type=MESH,
        )

    def send_group(t, _):
        other = (my_half + t + 1) % 2
        partner_group = other * half_groups + (my_group + t // 2) % half_groups

        def send_core(c, _):
            target = partner_group * group + (my_core + c) % group

            @pl.when(target != me)
            def _():
                for j in range(ACTIVE):
                    send[target, j] = store_ref[ids[target, 0, j]]
                piece_copy(target, me).start()

            return 0

        return lax.fori_loop(0, group, send_core, 0)

    lax.fori_loop(0, groups, send_group, 0)
    for j in range(ACTIVE):
        recv[me, j] = store_ref[ids[me, 0, j]]

    token_copy.wait()
    base_copy.wait()
    total[...] = jnp.zeros_like(total)
    wide[...] = jnp.zeros_like(wide)

    def base_step(g, _):
        at = pl.ds(pl.multiple_of(g * span, LANES), span)
        total[...] += jnp.dot(tokens[:, at], base[at, :], preferred_element_type=jnp.float32)
        return 0

    lax.fori_loop(0, groups, base_step, 0)

    rows = down_rows + up_rows
    twice = (
        lax.broadcasted_iota(jnp.int32, (2 * rows, rows), 0) // 2
        == lax.broadcasted_iota(jnp.int32, (2 * rows, rows), 1)
    ).astype(jnp.bfloat16)
    parity = (
        lax.broadcasted_iota(jnp.int32, (2 * rows, ACTIVE * LANES), 0) % 2
        == (lax.broadcasted_iota(jnp.int32, (2 * rows, ACTIVE * LANES), 1) % LANES) // R
    )

    def take_group(t, _):
        half = (my_half + t) % 2
        from_group = half * half_groups + (my_group - t // 2 + half_groups) % half_groups

        def take_core(c, _):
            origin = from_group * group + c

            @pl.when(origin != me)
            def _():
                piece_copy(origin, origin).wait_recv()

            packed = jnp.concatenate([recv[origin, j] for j in range(ACTIVE)], axis=1)
            spread = jnp.dot(twice, packed, preferred_element_type=jnp.float32)
            spread = jnp.where(parity, spread, 0.0)
            wide_weight[pl.ds(pl.multiple_of(c * d_local, 16), d_local), :] = spread[:d_local].astype(jnp.bfloat16)
            up_weight[pl.ds(pl.multiple_of(origin * 2 * up_rows, 8), 2 * up_rows), :] = spread[d_local:]
            return 0

        lax.fori_loop(0, group, take_core, 0)
        at = pl.ds(pl.multiple_of(from_group * span, LANES), span)
        wide[...] += jnp.dot(tokens[:, at], wide_weight[...], preferred_element_type=jnp.float32)
        return 0

    lax.fori_loop(0, groups, take_group, 0)

    position = lax.broadcasted_iota(jnp.int32, (row_count, LANES), 0)
    row_slot = jnp.zeros((row_count, LANES), jnp.int32)
    begin = jnp.int32(0)
    for p in range(lengths_ref.shape[1]):
        end = begin + lengths_ref[0, p]
        inside = jnp.logical_and(position >= begin, position < end)
        row_slot = jnp.where(inside, slots_ref[0, p], row_slot)
        begin = end
    picked = []
    for j in range(ACTIVE):
        mine = wide[:, j * LANES:(j + 1) * LANES]
        low = mine + pltpu.roll(mine, R, 1)
        picked.append(jnp.where(row_slot == j, low, 0.0).astype(jnp.bfloat16))
    low_rank = jnp.concatenate(picked, axis=1)
    delta = lax.dot_general(
        low_rank, up_weight[...].astype(jnp.bfloat16),
        (((1,), (1,)), ((), ())), preferred_element_type=jnp.float32,
    )
    out_ref[...] = (total[...] + adapter_scale * delta).astype(out_ref.dtype)

    def finish(k, _):
        target = (me + k) % n
        id_copy(k, me).wait_send()
        piece_copy(target, me).wait_send()
        return 0

    lax.fori_loop(1, n, finish, 0)


def chunks_of(tiles):
    bounds, at = [], 0
    for size in (3, 2, 2, 2, 1, 1):
        if at < tiles:
            bounds.append((at, min(tiles, at + size)))
            at += size
    if at < tiles:
        bounds.append((at, tiles))
    return bounds


def running_sum(counts):
    lane = lax.broadcasted_iota(jnp.int32, counts.shape, 1)
    shift = 1
    while shift < LANES:
        counts = counts + jnp.where(lane >= shift, pltpu.roll(counts, shift, 1), 0)
        shift *= 2
    return counts


def relay_kernel(
    n, part_count, down_rows, up_rows, capacity,
    active_ref, lengths_ref, slots_ref, tokens_hbm, base_hbm, store_ref, out_ref, flag_ref,
    tokens, base, ids_vmem, ids, place_vmem, place, list_vmem, id_list,
    far_send, send, recv, wide_weight, far_weight, up_weight, total, wide, flags, my_flag,
    id_send_sem, id_recv_sem, scalar_sem, far_send_sem, far_recv_sem, send_sem, own_send_sem, recv_sem,
    token_sem, base_sem, flag_send_sem, flag_recv_sem, *far,
):
    me = lax.axis_index("adapt")
    part = lax.axis_index("groups")
    d_local = 2 * down_rows
    rows = down_rows + up_rows
    tiles = store_ref.shape[0]
    pieces = chunks_of(tiles)
    half_n = n // 2
    plane_n = n // 4
    half = me // half_n
    other = 1 - half
    plane, within = me // plane_n, me % plane_n
    relays = plane == 1 + half
    relay_target = (1 + other) * plane_n + within
    group = LANES // math.gcd(LANES, d_local)
    half_groups = half_n // group
    span = group * d_local
    row_count = out_ref.shape[0]

    token_copy = pltpu.make_async_copy(tokens_hbm, tokens, token_sem)
    base_copy = pltpu.make_async_copy(base_hbm, base, base_sem)
    token_copy.start()
    base_copy.start()

    barrier = pltpu.get_barrier_semaphore()

    def greet(k, _):
        pl.semaphore_signal(
            barrier, inc=1, device_id={"groups": part, "adapt": (me + k) % n}, device_id_type=MESH)
        return 0

    def greet_part(k, _):
        pl.semaphore_signal(
            barrier, inc=1, device_id={"groups": (part + k) % part_count, "adapt": me}, device_id_type=MESH)
        return 0

    lax.fori_loop(1, n, greet, 0)
    lax.fori_loop(1, part_count, greet_part, 0)
    pl.semaphore_wait(barrier, n - 1 + part_count - 1)

    def id_copy(k, origin):
        return pltpu.make_async_remote_copy(
            src_ref=active_ref, dst_ref=ids_vmem.at[origin],
            send_sem=id_send_sem.at[k], recv_sem=id_recv_sem.at[origin],
            device_id={"groups": part, "adapt": (me + k) % n}, device_id_type=MESH,
        )

    def send_ids(k, _):
        id_copy(k, me).start()
        return 0

    def await_ids(k, _):
        id_copy(k, (me + k) % n).wait_recv()
        return 0

    lax.fori_loop(1, n, send_ids, 0)
    ids_vmem[me] = active_ref[...]
    lax.fori_loop(1, n, await_ids, 0)

    def ranks(which):
        theirs = ids_vmem[pl.ds(which * half_n, half_n)].reshape(half_n * 8, LANES)
        lane = lax.broadcasted_iota(jnp.int32, theirs.shape, 1)
        hit = (theirs == lane).astype(jnp.int32)
        present = jnp.broadcast_to(jnp.max(hit, axis=0, keepdims=True), (8, LANES))
        through = running_sum(present)
        return hit, present, through - present, jnp.max(through, axis=1, keepdims=True)

    _, far_present, far_rank, far_count = ranks(other)
    order = lax.broadcasted_iota(jnp.int32, (capacity, LANES), 0)
    number = lax.broadcasted_iota(jnp.int32, (capacity, LANES), 1)
    chosen = jnp.where((far_rank[0:1] == order) & (far_present[0:1] > 0), number, 0)
    list_vmem[...] = jnp.broadcast_to(jnp.sum(chosen, axis=1, keepdims=True), (capacity, LANES))
    hit, _, near_rank, near_count = ranks(half)
    spot = jnp.minimum(jnp.sum(hit * near_rank[0:1], axis=1, keepdims=True), capacity - 1)
    place_vmem[...] = jnp.broadcast_to(spot, (half_n * 8, LANES))
    my_flag[...] = jnp.broadcast_to(
        (jnp.maximum(far_count, near_count) > capacity).astype(jnp.int32), (8, LANES))

    scalar_copies = [
        pltpu.make_async_copy(list_vmem, id_list, scalar_sem.at[0]),
        pltpu.make_async_copy(ids_vmem, ids, scalar_sem.at[1]),
        pltpu.make_async_copy(place_vmem, place, scalar_sem.at[2]),
    ]
    for copy in scalar_copies:
        copy.start()
    for copy in scalar_copies:
        copy.wait()

    def far_copy(q, slot):
        low, high = pieces[q]
        return pltpu.make_async_remote_copy(
            src_ref=far_send.at[pl.ds(low, high - low)], dst_ref=far[q].at[slot],
            send_sem=far_send_sem.at[q], recv_sem=far_recv_sem.at[slot, q],
            device_id={"groups": part, "adapt": relay_target}, device_id_type=MESH,
        )

    for q, (low, high) in enumerate(pieces):
        def fill(k, _):
            for t in range(low, high):
                far_send[t, k] = store_ref[t, id_list[k, 0]]
            return 0

        lax.fori_loop(0, capacity, fill, 0)
        far_copy(q, plane % 2).start()

    def own_copy(d, origin):
        return pltpu.make_async_remote_copy(
            src_ref=send.at[2, d], dst_ref=recv.at[origin],
            send_sem=own_send_sem.at[d], recv_sem=recv_sem.at[origin, 0],
            device_id={"groups": part, "adapt": half * half_n + d}, device_id_type=MESH,
        )

    def send_own(k, _):
        d = (me + k) % half_n
        target = half * half_n + d
        for j in range(ACTIVE):
            for t in range(tiles):
                send[2, d, t, j] = store_ref[t, ids[target, j, 0]]
        own_copy(d, me).start()
        return 0

    lax.fori_loop(1, half_n, send_own, 0)
    for j in range(ACTIVE):
        for t in range(tiles):
            recv[me, t, j] = store_ref[t, ids[me, j, 0]]

    def part_copy(q, f, d, origin):
        low, high = pieces[q]
        return pltpu.make_async_remote_copy(
            src_ref=send.at[f, d, pl.ds(low, high - low)], dst_ref=recv.at[origin, pl.ds(low, high - low)],
            send_sem=send_sem.at[f, d, q], recv_sem=recv_sem.at[origin, q],
            device_id={"groups": part, "adapt": half * half_n + d}, device_id_type=MESH,
        )

    def far_origin(f):
        return (2 * other + f) * plane_n + within

    def relay(q):
        low, high = pieces[q]
        for f in range(2):
            far_copy(q, f).wait_recv()
        for f in range(2):
            def pass_on(k, _):
                d = (me + k) % half_n
                for j in range(ACTIVE):
                    for t in range(low, high):
                        send[f, d, t, j] = far[q][f, t - low, place[d * 8 + j, 0]]
                part_copy(q, f, d, far_origin(f)).start()
                return 0

            lax.fori_loop(1, half_n, pass_on, 0)
            for j in range(ACTIVE):
                for t in range(low, high):
                    recv[far_origin(f), t, j] = far[q][f, t - low, place[(me % half_n) * 8 + j, 0]]

    def spread_rows(origin, low, high):
        count = (high - low) * 16
        packed = jnp.concatenate(
            [recv[origin, low:high, j].reshape(count, LANES) for j in range(ACTIVE)], axis=1)
        twice = (
            lax.broadcasted_iota(jnp.int32, (2 * count, count), 0) // 2
            == lax.broadcasted_iota(jnp.int32, (2 * count, count), 1)
        ).astype(jnp.bfloat16)
        parity = (
            lax.broadcasted_iota(jnp.int32, (2 * count, ACTIVE * LANES), 0) % 2
            == (lax.broadcasted_iota(jnp.int32, (2 * count, ACTIVE * LANES), 1) % LANES) // R
        )
        return jnp.where(parity, jnp.dot(twice, packed, preferred_element_type=jnp.float32), 0.0)

    def place_rows(origin, low, high, target, offset):
        spread = spread_rows(origin, low, high)
        first, last = 32 * low, 32 * high
        if first < d_local:
            here = min(last, d_local) - first
            at = pl.ds(pl.multiple_of(offset + first, 16), here)
            target[at, :] = spread[:here].astype(jnp.bfloat16)
        if last > d_local:
            begin = max(first, d_local)
            end = min(last, 2 * rows)
            at = pl.ds(pl.multiple_of(origin * 2 * up_rows + begin - d_local, 8), end - begin)
            up_weight[at, :] = spread[begin - first:end - first]

    def base_step(g, _):
        at = pl.ds(pl.multiple_of(g * span, LANES), span)
        total[...] += jnp.dot(tokens[:, at], base[at, :], preferred_element_type=jnp.float32)
        return 0

    def near_step(g, _):
        from_group = half * half_groups + (me % half_n // group + g) % half_groups

        def take_core(c, _):
            origin = from_group * group + c

            @pl.when(origin != me)
            def _():
                own_copy(me % half_n, origin).wait_recv()

            place_rows(origin, 0, tiles, wide_weight, c * d_local)
            return 0

        lax.fori_loop(0, group, take_core, 0)
        at = pl.ds(pl.multiple_of(from_group * span, LANES), span)
        wide[...] += jnp.dot(tokens[:, at], wide_weight[...], preferred_element_type=jnp.float32)
        return 0

    def take_far(q):
        low, high = pieces[q]

        def take_one(k, _):
            origin = other * half_n + k
            passed = (1 + half) * plane_n + k % plane_n

            @pl.when(passed != me)
            def _():
                part_copy(q, 0, me % half_n, origin).wait_recv()

            place_rows(origin, low, high, far_weight, k * d_local)
            return 0

        lax.fori_loop(0, half_n, take_one, 0)

    token_copy.wait()
    base_copy.wait()
    total[...] = jnp.zeros_like(total)
    wide[...] = jnp.zeros_like(wide)
    steps = len(pieces)
    for q in range(steps):
        @pl.when(relays)
        def _():
            relay(q)

        low, high = 2 * half_groups * q // steps, 2 * half_groups * (q + 1) // steps
        lax.fori_loop(low, high, base_step, 0)
        low, high = half_groups * q // steps, half_groups * (q + 1) // steps
        lax.fori_loop(low, high, near_step, 0)
        if q >= 1:
            take_far(q - 1)
    take_far(steps - 1)

    def far_step(g, _):
        at = pl.ds(pl.multiple_of(other * half_n * d_local + g * span, LANES), span)
        of = pl.ds(pl.multiple_of(g * span, LANES), span)
        wide[...] += jnp.dot(tokens[:, at], far_weight[of, :], preferred_element_type=jnp.float32)
        return 0

    lax.fori_loop(0, half_groups, far_step, 0)

    position = lax.broadcasted_iota(jnp.int32, (row_count, LANES), 0)
    row_slot = jnp.zeros((row_count, LANES), jnp.int32)
    begin = jnp.int32(0)
    for p in range(lengths_ref.shape[1]):
        end = begin + lengths_ref[0, p]
        inside = jnp.logical_and(position >= begin, position < end)
        row_slot = jnp.where(inside, slots_ref[0, p], row_slot)
        begin = end
    picked = []
    for j in range(ACTIVE):
        mine = wide[:, j * LANES:(j + 1) * LANES]
        low_rank = mine + pltpu.roll(mine, R, 1)
        picked.append(jnp.where(row_slot == j, low_rank, 0.0).astype(jnp.bfloat16))
    delta = lax.dot_general(
        jnp.concatenate(picked, axis=1), up_weight[...].astype(jnp.bfloat16),
        (((1,), (1,)), ((), ())), preferred_element_type=jnp.float32,
    )
    out_ref[...] = (total[...] + adapter_scale * delta).astype(out_ref.dtype)

    def flag_copy(k, origin):
        return pltpu.make_async_remote_copy(
            src_ref=my_flag, dst_ref=flags.at[origin],
            send_sem=flag_send_sem.at[k], recv_sem=flag_recv_sem.at[origin],
            device_id={"groups": (part + k) % part_count, "adapt": me}, device_id_type=MESH,
        )

    def send_flag(k, _):
        flag_copy(k, part).start()
        return 0

    def await_flag(k, _):
        flag_copy(k, (part + k) % part_count).wait_recv()
        flag_copy(k, part).wait_send()
        return 0

    lax.fori_loop(1, part_count, send_flag, 0)
    flags[part] = my_flag[...]

    def finish(k, _):
        id_copy(k, me).wait_send()
        return 0

    def finish_near(k, _):
        own_copy((me + k) % half_n, me).wait_send()
        return 0

    lax.fori_loop(1, n, finish, 0)
    lax.fori_loop(1, half_n, finish_near, 0)
    for q in range(steps):
        far_copy(q, plane % 2).wait_send()

    @pl.when(relays)
    def _():
        for q in range(steps):
            for f in range(2):
                def finish_part(k, _):
                    part_copy(q, f, (me + k) % half_n, far_origin(f)).wait_send()
                    return 0

                lax.fori_loop(1, half_n, finish_part, 0)

    lax.fori_loop(1, part_count, await_flag, 0)
    flag_ref[...] = jnp.max(flags[...], axis=0)


def direct(slot_list, lengths, program_adapter_slot, tokens, base_weight, store, down_rows, up_rows):
    n = lax.axis_size("adapt")
    row_count = tokens.shape[0]
    rows = down_rows + up_rows
    d_local = 2 * down_rows
    group = LANES // math.gcd(LANES, d_local)
    vmem, smem, hbm = pltpu.VMEM, pltpu.SMEM, pl.ANY
    width = ACTIVE * LANES
    return pl.pallas_call(
        functools.partial(direct_kernel, n, down_rows, up_rows),
        out_shape=jax.ShapeDtypeStruct((row_count, KV), jnp.bfloat16),
        in_specs=[pl.BlockSpec(memory_space=s) for s in (vmem, smem, smem, hbm, hbm, vmem)],
        out_specs=pl.BlockSpec(memory_space=vmem),
        scratch_shapes=[
            pltpu.VMEM((row_count, D), jnp.bfloat16),
            pltpu.VMEM((D, KV), jnp.bfloat16),
            pltpu.VMEM((n, 1, LANES), jnp.int32),
            pltpu.SMEM((n, 1, LANES), jnp.int32),
            pltpu.VMEM((n, ACTIVE, rows, LANES), jnp.bfloat16),
            pltpu.VMEM((n, ACTIVE, rows, LANES), jnp.bfloat16),
            pltpu.VMEM((group * d_local, width), jnp.bfloat16),
            pltpu.VMEM((KV, width), jnp.float32),
            pltpu.VMEM((row_count, KV), jnp.float32),
            pltpu.VMEM((row_count, width), jnp.float32),
            pltpu.SemaphoreType.DMA((n,)),
            pltpu.SemaphoreType.DMA((n,)),
            pltpu.SemaphoreType.DMA,
            pltpu.SemaphoreType.DMA((n,)),
            pltpu.SemaphoreType.DMA((n,)),
            pltpu.SemaphoreType.DMA,
            pltpu.SemaphoreType.DMA,
        ],
        compiler_params=pltpu.CompilerParams(
            collective_id=1, has_side_effects=True, vmem_limit_bytes=48 * 1024 * 1024
        ),
    )(slot_list, lengths, program_adapter_slot, tokens, base_weight, store)


def shards(tokens, lengths, active, program_adapter_slot, base_weight, adapter_down, adapter_up):
    n = lax.axis_size("adapt")
    part_count = lax.axis_size("groups")
    row_count = tokens.shape[0]
    stored = adapter_down.shape[0]
    down_rows = adapter_down.shape[1] // LANES
    up_rows = adapter_up.shape[1] // LANES
    rows = down_rows + up_rows
    tiles = -(-rows // 16)
    both = jnp.concatenate([adapter_down, adapter_up], axis=1)
    store = jnp.pad(both, ((0, 0), (0, (16 * tiles - rows) * LANES)))
    store = store.reshape(stored, tiles, 16, LANES).transpose(1, 0, 2, 3)
    slot_rows = jnp.broadcast_to(active.reshape(ACTIVE, 1), (ACTIVE, LANES))
    slot_rows = jnp.pad(slot_rows, ((0, 8 - ACTIVE), (0, 0)), constant_values=-1)
    d_local = 2 * down_rows
    group = LANES // math.gcd(LANES, d_local)
    half_n = n // 2
    capacity = 3 * min(stored, half_n * ACTIVE) // 4
    steps = len(chunks_of(tiles))
    width = ACTIVE * LANES
    vmem, smem, hbm = pltpu.VMEM, pltpu.SMEM, pl.ANY
    dma = pltpu.SemaphoreType.DMA
    values, flag = pl.pallas_call(
        functools.partial(relay_kernel, n, part_count, down_rows, up_rows, capacity),
        out_shape=(
            jax.ShapeDtypeStruct((row_count, KV), jnp.bfloat16),
            jax.ShapeDtypeStruct((8, LANES), jnp.int32),
        ),
        in_specs=[pl.BlockSpec(memory_space=s) for s in (vmem, smem, smem, hbm, hbm, vmem)],
        out_specs=(pl.BlockSpec(memory_space=vmem), pl.BlockSpec(memory_space=vmem)),
        scratch_shapes=[
            pltpu.VMEM((row_count, D), jnp.bfloat16),
            pltpu.VMEM((D, KV), jnp.bfloat16),
            pltpu.VMEM((n, 8, LANES), jnp.int32),
            pltpu.SMEM((n, 8, LANES), jnp.int32),
            pltpu.VMEM((half_n * 8, LANES), jnp.int32),
            pltpu.SMEM((half_n * 8, LANES), jnp.int32),
            pltpu.VMEM((capacity, LANES), jnp.int32),
            pltpu.SMEM((capacity, LANES), jnp.int32),
            pltpu.VMEM((tiles, capacity, 16, LANES), jnp.bfloat16),
            pltpu.VMEM((3, half_n, tiles, ACTIVE, 16, LANES), jnp.bfloat16),
            pltpu.VMEM((n, tiles, ACTIVE, 16, LANES), jnp.bfloat16),
            pltpu.VMEM((group * d_local, width), jnp.bfloat16),
            pltpu.VMEM((half_n * d_local, width), jnp.bfloat16),
            pltpu.VMEM((KV, width), jnp.float32),
            pltpu.VMEM((row_count, KV), jnp.float32),
            pltpu.VMEM((row_count, width), jnp.float32),
            pltpu.VMEM((part_count, 8, LANES), jnp.int32),
            pltpu.VMEM((8, LANES), jnp.int32),
            dma((n,)), dma((n,)), dma((3,)), dma((steps,)), dma((2, steps)),
            dma((2, half_n, steps)), dma((half_n,)), dma((n, steps)),
            dma, dma, dma((part_count,)), dma((part_count,)),
        ] + [
            pltpu.VMEM((2, high - low, capacity, 16, LANES), jnp.bfloat16)
            for low, high in chunks_of(tiles)
        ],
        compiler_params=pltpu.CompilerParams(
            collective_id=0, has_side_effects=True, vmem_limit_bytes=56 * 1024 * 1024
        ),
    )(slot_rows, lengths, program_adapter_slot, tokens, base_weight, store)

    def over(_):
        slot_list = jnp.pad(active, ((0, 0), (0, LANES - ACTIVE)))
        return direct(
            slot_list, lengths, program_adapter_slot, tokens, base_weight,
            both.reshape(stored, rows, LANES), down_rows, up_rows)

    return lax.cond(flag[0, 0] > 0, over, lambda ready: ready, values)


def solution(mesh):
    in_specs = (
        P(("groups", "adapt"), None),
        P(("groups", "adapt"), None),
        P(("groups", "adapt"), None),
        P(("groups", "adapt"), None),
        P(),
        P("groups", "adapt"),
        P("groups", "adapt"),
    )
    out_specs = P(("groups", "adapt"), None)
    return jax.shard_map(shards, mesh=mesh, in_specs=in_specs, out_specs=out_specs, check_vma=False)
```

```python
import functools
import math

import jax
import jax.numpy as jnp
from jax import lax
from jax.experimental import pallas as pl
from jax.experimental.pallas import tpu as pltpu
from jax.sharding import PartitionSpec as P

D = 5120
KV = 512
R = 64
ACTIVE = 4
LANES = 128

adapter_scale = 2.0
MESH = pl.DeviceIdType.MESH


def kernel(
    n, down_rows, up_rows,
    active_ref, lengths_ref, slots_ref, tokens_hbm, base_hbm, store_ref, out_ref,
    tokens, base, ids_vmem, ids, send, recv, wide_weight, up_weight, total, wide,
    id_send_sem, id_recv_sem, id_sem, send_sem, recv_sem, token_sem, base_sem,
):
    me = lax.axis_index("adapt")
    d_local = 2 * down_rows
    group = LANES // math.gcd(LANES, d_local)
    groups = n // group
    half_groups = groups // 2
    span = group * d_local
    my_group, my_core = me // group, me % group
    my_half = my_group // half_groups
    row_count = out_ref.shape[0]

    token_copy = pltpu.make_async_copy(tokens_hbm, tokens, token_sem)
    base_copy = pltpu.make_async_copy(base_hbm, base, base_sem)
    token_copy.start()
    base_copy.start()

    barrier = pltpu.get_barrier_semaphore()

    def greet(k, _):
        pl.semaphore_signal(barrier, inc=1, device_id={"adapt": (me + k) % n}, device_id_type=MESH)
        return 0

    lax.fori_loop(1, n, greet, 0)
    pl.semaphore_wait(barrier, n - 1)

    def id_copy(k, origin):
        return pltpu.make_async_remote_copy(
            src_ref=active_ref, dst_ref=ids_vmem.at[origin],
            send_sem=id_send_sem.at[k], recv_sem=id_recv_sem.at[origin],
            device_id={"adapt": (me + k) % n}, device_id_type=MESH,
        )

    def send_ids(k, _):
        id_copy(k, me).start()
        return 0

    def await_ids(k, _):
        id_copy(k, (me + k) % n).wait_recv()
        return 0

    lax.fori_loop(1, n, send_ids, 0)
    ids_vmem[me] = active_ref[...]
    lax.fori_loop(1, n, await_ids, 0)
    to_scalars = pltpu.make_async_copy(ids_vmem, ids, id_sem)
    to_scalars.start()
    to_scalars.wait()

    def piece_copy(target, origin):
        return pltpu.make_async_remote_copy(
            src_ref=send.at[target], dst_ref=recv.at[origin],
            send_sem=send_sem.at[target], recv_sem=recv_sem.at[origin],
            device_id={"adapt": target}, device_id_type=MESH,
        )

    def send_group(t, _):
        other = (my_half + t + 1) % 2
        partner_group = other * half_groups + (my_group + t // 2) % half_groups

        def send_core(c, _):
            target = partner_group * group + (my_core + c) % group

            @pl.when(target != me)
            def _():
                for j in range(ACTIVE):
                    send[target, j] = store_ref[ids[target, 0, j]]

            @pl.when(jnp.logical_and(target != me, jnp.logical_or(t % 2 == 1, t < 4)))
            def _():
                piece_copy(target, me).start()

            return 0

        return lax.fori_loop(0, group, send_core, 0)

    lax.fori_loop(0, groups, send_group, 0)
    for j in range(ACTIVE):
        recv[me, j] = store_ref[ids[me, 0, j]]

    token_copy.wait()
    base_copy.wait()
    total[...] = jnp.zeros_like(total)
    wide[...] = jnp.zeros_like(wide)

    def base_step(g, _):
        at = pl.ds(pl.multiple_of(g * span, LANES), span)
        total[...] += jnp.dot(tokens[:, at], base[at, :], preferred_element_type=jnp.float32)
        return 0

    lax.fori_loop(0, groups, base_step, 0)

    rows = down_rows + up_rows
    twice = (
        lax.broadcasted_iota(jnp.int32, (2 * rows, rows), 0) // 2
        == lax.broadcasted_iota(jnp.int32, (2 * rows, rows), 1)
    ).astype(jnp.bfloat16)
    parity = (
        lax.broadcasted_iota(jnp.int32, (2 * rows, ACTIVE * LANES), 0) % 2
        == (lax.broadcasted_iota(jnp.int32, (2 * rows, ACTIVE * LANES), 1) % LANES) // R
    )

    def take_group(t, _):
        half = (my_half + t) % 2
        from_group = half * half_groups + (my_group - t // 2 + half_groups) % half_groups

        def take_core(c, _):
            origin = from_group * group + c

            @pl.when(origin != me)
            def _():
                piece_copy(origin, origin).wait_recv()

            packed = jnp.concatenate([recv[origin, j] for j in range(ACTIVE)], axis=1)
            spread = jnp.dot(twice, packed, preferred_element_type=jnp.float32)
            spread = jnp.where(parity, spread, 0.0)
            wide_weight[pl.ds(pl.multiple_of(c * d_local, 16), d_local), :] = spread[:d_local].astype(jnp.bfloat16)
            up_weight[pl.ds(pl.multiple_of(origin * 2 * up_rows, 8), 2 * up_rows), :] = spread[d_local:]
            return 0

        lax.fori_loop(0, group, take_core, 0)
        at = pl.ds(pl.multiple_of(from_group * span, LANES), span)
        wide[...] += jnp.dot(tokens[:, at], wide_weight[...], preferred_element_type=jnp.float32)
        return 0

    def far_target(q, c):
        partner_group = (1 - my_half) * half_groups + (my_group + q) % half_groups
        return partner_group * group + (my_core + c) % group

    def take_near(q, _):
        return take_group(2 * q, 0)

    def take_far(q, _):
        def sent(c, _):
            piece_copy(far_target(q, c), me).wait_send()
            return 0

        def start_later(c, _):
            piece_copy(far_target(q + 2, c), me).start()
            return 0

        lax.fori_loop(0, group, sent, 0)

        @pl.when(q + 2 < half_groups)
        def _():
            lax.fori_loop(0, group, start_later, 0)

        return take_group(2 * q + 1, 0)

    lax.fori_loop(0, half_groups, take_near, 0)
    lax.fori_loop(0, half_groups, take_far, 0)

    position = lax.broadcasted_iota(jnp.int32, (row_count, LANES), 0)
    row_slot = jnp.zeros((row_count, LANES), jnp.int32)
    begin = jnp.int32(0)
    for p in range(lengths_ref.shape[1]):
        end = begin + lengths_ref[0, p]
        inside = jnp.logical_and(position >= begin, position < end)
        row_slot = jnp.where(inside, slots_ref[0, p], row_slot)
        begin = end
    picked = []
    for j in range(ACTIVE):
        mine = wide[:, j * LANES:(j + 1) * LANES]
        low = mine + pltpu.roll(mine, R, 1)
        picked.append(jnp.where(row_slot == j, low, 0.0).astype(jnp.bfloat16))
    low_rank = jnp.concatenate(picked, axis=1)
    delta = lax.dot_general(
        low_rank, up_weight[...].astype(jnp.bfloat16),
        (((1,), (1,)), ((), ())), preferred_element_type=jnp.float32,
    )
    out_ref[...] = (total[...] + adapter_scale * delta).astype(out_ref.dtype)

    def finish(k, _):
        id_copy(k, me).wait_send()
        return 0

    def finish_near(k, _):
        half_n = n // 2
        piece_copy(my_half * half_n + (me + k) % half_n, me).wait_send()
        return 0

    lax.fori_loop(1, n, finish, 0)
    lax.fori_loop(1, n // 2, finish_near, 0)


def shards(tokens, lengths, active, program_adapter_slot, base_weight, adapter_down, adapter_up):
    n = lax.axis_size("adapt")
    row_count = tokens.shape[0]
    stored = adapter_down.shape[0]
    down_rows = adapter_down.shape[1] // LANES
    up_rows = adapter_up.shape[1] // LANES
    rows = down_rows + up_rows
    store = jnp.concatenate([adapter_down, adapter_up], axis=1).reshape(stored, rows, LANES)
    slot_list = jnp.pad(active, ((0, 0), (0, LANES - ACTIVE)))
    d_local = 2 * down_rows
    group = LANES // math.gcd(LANES, d_local)
    vmem, smem, hbm = pltpu.VMEM, pltpu.SMEM, pl.ANY
    width = ACTIVE * LANES
    return pl.pallas_call(
        functools.partial(kernel, n, down_rows, up_rows),
        out_shape=jax.ShapeDtypeStruct((row_count, KV), jnp.bfloat16),
        in_specs=[pl.BlockSpec(memory_space=s) for s in (vmem, smem, smem, hbm, hbm, vmem)],
        out_specs=pl.BlockSpec(memory_space=vmem),
        scratch_shapes=[
            pltpu.VMEM((row_count, D), jnp.bfloat16),
            pltpu.VMEM((D, KV), jnp.bfloat16),
            pltpu.VMEM((n, 1, LANES), jnp.int32),
            pltpu.SMEM((n, 1, LANES), jnp.int32),
            pltpu.VMEM((n, ACTIVE, rows, LANES), jnp.bfloat16),
            pltpu.VMEM((n, ACTIVE, rows, LANES), jnp.bfloat16),
            pltpu.VMEM((group * d_local, width), jnp.bfloat16),
            pltpu.VMEM((KV, width), jnp.float32),
            pltpu.VMEM((row_count, KV), jnp.float32),
            pltpu.VMEM((row_count, width), jnp.float32),
            pltpu.SemaphoreType.DMA((n,)),
            pltpu.SemaphoreType.DMA((n,)),
            pltpu.SemaphoreType.DMA,
            pltpu.SemaphoreType.DMA((n,)),
            pltpu.SemaphoreType.DMA((n,)),
            pltpu.SemaphoreType.DMA,
            pltpu.SemaphoreType.DMA,
        ],
        compiler_params=pltpu.CompilerParams(
            collective_id=0, has_side_effects=True, vmem_limit_bytes=48 * 1024 * 1024
        ),
    )(slot_list, lengths, program_adapter_slot, tokens, base_weight, store)


def solution(mesh):
    in_specs = (
        P(("groups", "adapt"), None),
        P(("groups", "adapt"), None),
        P(("groups", "adapt"), None),
        P(("groups", "adapt"), None),
        P(),
        P("groups", "adapt"),
        P("groups", "adapt"),
    )
    out_specs = P(("groups", "adapt"), None)
    return jax.shard_map(shards, mesh=mesh, in_specs=in_specs, out_specs=out_specs, check_vma=False)
```

```python
import functools
import math

import jax
import jax.numpy as jnp
from jax import lax
from jax.experimental import pallas as pl
from jax.experimental.pallas import tpu as pltpu
from jax.sharding import PartitionSpec as P

D = 5120
KV = 512
R = 64
ACTIVE = 4
LANES = 128

adapter_scale = 2.0
MESH = pl.DeviceIdType.MESH


def kernel(
    n, down_rows, up_rows,
    active_ref, lengths_ref, slots_ref, tokens_hbm, base_hbm, store_ref, out_ref,
    tokens, base, ids_vmem, ids, send, recv, wide_weight, up_weight, total, wide,
    id_send_sem, id_recv_sem, id_sem, send_sem, recv_sem, token_sem, base_sem,
):
    me = lax.axis_index("adapt")
    d_local = 2 * down_rows
    group = LANES // math.gcd(LANES, d_local)
    groups = n // group
    half_groups = groups // 2
    span = group * d_local
    my_group, my_core = me // group, me % group
    my_half = my_group // half_groups
    row_count = out_ref.shape[0]

    token_copy = pltpu.make_async_copy(tokens_hbm, tokens, token_sem)
    base_copy = pltpu.make_async_copy(base_hbm, base, base_sem)
    token_copy.start()
    base_copy.start()

    barrier = pltpu.get_barrier_semaphore()

    def greet(k, _):
        pl.semaphore_signal(barrier, inc=1, device_id={"adapt": (me + k) % n}, device_id_type=MESH)
        return 0

    lax.fori_loop(1, n, greet, 0)
    pl.semaphore_wait(barrier, n - 1)

    def id_copy(k, origin):
        return pltpu.make_async_remote_copy(
            src_ref=active_ref, dst_ref=ids_vmem.at[origin],
            send_sem=id_send_sem.at[k], recv_sem=id_recv_sem.at[origin],
            device_id={"adapt": (me + k) % n}, device_id_type=MESH,
        )

    def send_ids(k, _):
        id_copy(k, me).start()
        return 0

    def await_ids(k, _):
        id_copy(k, (me + k) % n).wait_recv()
        return 0

    lax.fori_loop(1, n, send_ids, 0)
    ids_vmem[me] = active_ref[...]
    lax.fori_loop(1, n, await_ids, 0)
    to_scalars = pltpu.make_async_copy(ids_vmem, ids, id_sem)
    to_scalars.start()
    to_scalars.wait()

    def piece_copy(target, origin):
        return pltpu.make_async_remote_copy(
            src_ref=send.at[target], dst_ref=recv.at[origin],
            send_sem=send_sem.at[target], recv_sem=recv_sem.at[origin],
            device_id={"adapt": target}, device_id_type=MESH,
        )

    def send_group(t, _):
        other = (my_half + t + 1) % 2
        partner_group = other * half_groups + (my_group + t // 2) % half_groups

        def send_core(c, _):
            target = partner_group * group + (my_core + c) % group

            @pl.when(target != me)
            def _():
                for j in range(ACTIVE):
                    send[target, j] = store_ref[ids[target, 0, j]]
                piece_copy(target, me).start()

            return 0

        return lax.fori_loop(0, group, send_core, 0)

    lax.fori_loop(0, groups, send_group, 0)
    for j in range(ACTIVE):
        recv[me, j] = store_ref[ids[me, 0, j]]

    token_copy.wait()
    base_copy.wait()
    total[...] = jnp.zeros_like(total)
    wide[...] = jnp.zeros_like(wide)

    def base_step(g, _):
        at = pl.ds(pl.multiple_of(g * span, LANES), span)
        total[...] += jnp.dot(tokens[:, at], base[at, :], preferred_element_type=jnp.float32)
        return 0

    lax.fori_loop(0, groups, base_step, 0)

    rows = down_rows + up_rows
    twice = (
        lax.broadcasted_iota(jnp.int32, (2 * rows, rows), 0) // 2
        == lax.broadcasted_iota(jnp.int32, (2 * rows, rows), 1)
    ).astype(jnp.bfloat16)
    parity = (
        lax.broadcasted_iota(jnp.int32, (2 * rows, ACTIVE * LANES), 0) % 2
        == (lax.broadcasted_iota(jnp.int32, (2 * rows, ACTIVE * LANES), 1) % LANES) // R
    )

    def take_group(t, _):
        half = (my_half + t // half_groups) % 2
        from_group = half * half_groups + (my_group - t % half_groups + half_groups) % half_groups

        def take_core(c, _):
            origin = from_group * group + c

            @pl.when(origin != me)
            def _():
                piece_copy(origin, origin).wait_recv()

            packed = jnp.concatenate([recv[origin, j] for j in range(ACTIVE)], axis=1)
            spread = jnp.dot(twice, packed, preferred_element_type=jnp.float32)
            spread = jnp.where(parity, spread, 0.0)
            wide_weight[pl.ds(pl.multiple_of(c * d_local, 16), d_local), :] = spread[:d_local].astype(jnp.bfloat16)
            up_weight[pl.ds(pl.multiple_of(origin * 2 * up_rows, 8), 2 * up_rows), :] = spread[d_local:]
            return 0

        lax.fori_loop(0, group, take_core, 0)
        at = pl.ds(pl.multiple_of(from_group * span, LANES), span)
        wide[...] += jnp.dot(tokens[:, at], wide_weight[...], preferred_element_type=jnp.float32)
        return 0

    lax.fori_loop(0, groups, take_group, 0)

    position = lax.broadcasted_iota(jnp.int32, (row_count, LANES), 0)
    row_slot = jnp.zeros((row_count, LANES), jnp.int32)
    begin = jnp.int32(0)
    for p in range(lengths_ref.shape[1]):
        end = begin + lengths_ref[0, p]
        inside = jnp.logical_and(position >= begin, position < end)
        row_slot = jnp.where(inside, slots_ref[0, p], row_slot)
        begin = end
    picked = []
    for j in range(ACTIVE):
        mine = wide[:, j * LANES:(j + 1) * LANES]
        low = mine + pltpu.roll(mine, R, 1)
        picked.append(jnp.where(row_slot == j, low, 0.0).astype(jnp.bfloat16))
    low_rank = jnp.concatenate(picked, axis=1)
    delta = lax.dot_general(
        low_rank, up_weight[...].astype(jnp.bfloat16),
        (((1,), (1,)), ((), ())), preferred_element_type=jnp.float32,
    )
    out_ref[...] = (total[...] + adapter_scale * delta).astype(out_ref.dtype)

    def finish(k, _):
        target = (me + k) % n
        id_copy(k, me).wait_send()
        piece_copy(target, me).wait_send()
        return 0

    lax.fori_loop(1, n, finish, 0)


def shards(tokens, lengths, active, program_adapter_slot, base_weight, adapter_down, adapter_up):
    n = lax.axis_size("adapt")
    row_count = tokens.shape[0]
    stored = adapter_down.shape[0]
    down_rows = adapter_down.shape[1] // LANES
    up_rows = adapter_up.shape[1] // LANES
    rows = down_rows + up_rows
    store = jnp.concatenate([adapter_down, adapter_up], axis=1).reshape(stored, rows, LANES)
    slot_list = jnp.pad(active, ((0, 0), (0, LANES - ACTIVE)))
    d_local = 2 * down_rows
    group = LANES // math.gcd(LANES, d_local)
    vmem, smem, hbm = pltpu.VMEM, pltpu.SMEM, pl.ANY
    width = ACTIVE * LANES
    return pl.pallas_call(
        functools.partial(kernel, n, down_rows, up_rows),
        out_shape=jax.ShapeDtypeStruct((row_count, KV), jnp.bfloat16),
        in_specs=[pl.BlockSpec(memory_space=s) for s in (vmem, smem, smem, hbm, hbm, vmem)],
        out_specs=pl.BlockSpec(memory_space=vmem),
        scratch_shapes=[
            pltpu.VMEM((row_count, D), jnp.bfloat16),
            pltpu.VMEM((D, KV), jnp.bfloat16),
            pltpu.VMEM((n, 1, LANES), jnp.int32),
            pltpu.SMEM((n, 1, LANES), jnp.int32),
            pltpu.VMEM((n, ACTIVE, rows, LANES), jnp.bfloat16),
            pltpu.VMEM((n, ACTIVE, rows, LANES), jnp.bfloat16),
            pltpu.VMEM((group * d_local, width), jnp.bfloat16),
            pltpu.VMEM((KV, width), jnp.float32),
            pltpu.VMEM((row_count, KV), jnp.float32),
            pltpu.VMEM((row_count, width), jnp.float32),
            pltpu.SemaphoreType.DMA((n,)),
            pltpu.SemaphoreType.DMA((n,)),
            pltpu.SemaphoreType.DMA,
            pltpu.SemaphoreType.DMA((n,)),
            pltpu.SemaphoreType.DMA((n,)),
            pltpu.SemaphoreType.DMA,
            pltpu.SemaphoreType.DMA,
        ],
        compiler_params=pltpu.CompilerParams(
            collective_id=0, has_side_effects=True, vmem_limit_bytes=48 * 1024 * 1024
        ),
    )(slot_list, lengths, program_adapter_slot, tokens, base_weight, store)


def solution(mesh):
    in_specs = (
        P(("groups", "adapt"), None),
        P(("groups", "adapt"), None),
        P(("groups", "adapt"), None),
        P(("groups", "adapt"), None),
        P(),
        P("groups", "adapt"),
        P("groups", "adapt"),
    )
    out_specs = P(("groups", "adapt"), None)
    return jax.shard_map(shards, mesh=mesh, in_specs=in_specs, out_specs=out_specs, check_vma=False)
```
